512 devices in a mesh: group: 8 (over z_lo, core), ctx: 64 (over x, y, z_hi).
Axes of the slice: x: 4, y: 4, z: 16 (z_hi: 4, z_lo: 4; z = z_hi * 4 + z_lo), core: 2. Of those that a mesh axis runs over, the one named last changes fastest.
Arguments:
- queries: bfloat16 [8192, 4096], P(('group', 'ctx')), may hold values from -16 to 16
- key_states: bfloat16 [8192, 4096], P(('group', 'ctx')), may hold values from -16 to 16
- value_states: bfloat16 [8192, 4096], P(('group', 'ctx')), may hold values from -6 to 6
- gate_table: float32 [32, 4096], replicated, may hold values from 0.3 to 3
- noise_levels: int32 [8], replicated, may hold values from 0 to 31
- group_ids: int32 [8], replicated, may hold values from 0 to 7, each once
Outputs:
- handed: bfloat16 [8192, 4096], P(('group', 'ctx'))
The draws below stay inside these ranges and needn't reach their ends.
Inputs may be any that keep to these rules, and one draw needn't show every extreme that they name: `group_ids`: each of 0 to 7 appears once.
All inputs are finite; a program needn't handle non-finite values.
Results may differ from the reference program's by a relative error of at most 0.007.
Values may be sent and summed in bfloat16 or wider, within the bound.
A program may use at most 64 MiB of HBM per device.

```python
import math
import jax
import jax.numpy as jnp
from jax import lax

HEADS = 32
HEAD = 128
LEVELS = 32
GROUPS = 8
GROUP_TOK = 1024
TOKENS = 8192


def draw_queries(key, part):
    key = jax.random.fold_in(key, 11)
    base = jnp.clip(jax.random.normal(key, (TOKENS, HEADS * HEAD), jnp.float32), -5.0, 5.0)
    return base.astype(jnp.bfloat16)


def draw_key_states(key, part):
    key = jax.random.fold_in(key, 23)
    base = jnp.clip(jax.random.normal(key, (TOKENS, HEADS * HEAD), jnp.float32), -5.0, 5.0)
    return base.astype(jnp.bfloat16)


def touch_ends(array, rng, low, high):
    extent = array.shape
    spot = [jax.random.randint(jax.random.fold_in(rng, axis), (), 0, extent[axis]) for axis in range(len(extent))]
    array = array.at[tuple(spot)].set(low)
    longest = extent.index(max(extent))
    spot[longest] = (spot[longest] + 1) % extent[longest]
    return array.at[tuple(spot)].set(high)


def level_of(stream_key, dims, split, least, high):
    factor_of, own = 1.0, jax.random.fold_in(stream_key, 6)
    for dim, parts in split:
        draws = jnp.exp(jax.random.uniform(jax.random.fold_in(own, dim), (parts,), jnp.float32, least / len(split), high / len(split)))
        factor_of = factor_of * jnp.repeat(draws, dims[dim] // parts).reshape([-1 if axis == dim else 1 for axis in range(len(dims))])
    return factor_of


def scatter_about(own_key, extent, width, most, cuts=(), held_as=jnp.bfloat16):
    drawn = jax.random.normal(own_key, extent, jnp.float32) * width
    if len(cuts) > 0:
        drawn = level_of(own_key, extent, cuts, -0.22, 0.18) * drawn
    return jnp.clip(drawn, min=-most, max=most).astype(held_as)


def setup_inputs(seed: int = 0) -> dict:
    streams_of = jax.random.split(jax.random.key(seed), 7)
    return {
        "queries": draw_queries(jax.random.fold_in(streams_of[6], 71), 0),
        "key_states": draw_key_states(jax.random.fold_in(streams_of[6], 71), 0),
        "value_states": scatter_about(streams_of[2], (TOKENS, HEADS * HEAD), 1.0, 6.0, ((0, 512),)),
        "gate_table": jnp.clip(jnp.exp(jax.random.uniform(streams_of[3], (LEVELS, HEADS * HEAD), jnp.float32, math.log(0.3), math.log(3.0))), 0.3, 3.0),
        "noise_levels": touch_ends(jax.random.randint(streams_of[4], (GROUPS,), 0, LEVELS), jax.random.fold_in(streams_of[4], 1), 0, LEVELS - 1).astype(jnp.int32),
        "group_ids": jax.random.permutation(streams_of[5], GROUPS).astype(jnp.int32),
    }


def reference(queries, key_states, value_states, gate_table, noise_levels, group_ids):
    score_scale = 1.0 / (HEAD ** 0.5)
    query_grid = queries.reshape(GROUPS, GROUP_TOK, HEADS, HEAD)
    key_grid = key_states.reshape(TOKENS, HEADS, HEAD)
    value_grid = value_states.reshape(TOKENS, HEADS, HEAD)
    key_ids = jnp.repeat(group_ids, GROUP_TOK)

    def one_head(index_pair):
        group_index, head_index = index_pair
        query_head = query_grid[group_index, :, head_index, :].astype(jnp.float32)
        key_head = key_grid[:, head_index, :].astype(jnp.float32)
        value_head = value_grid[:, head_index, :]
        scores = jnp.dot(query_head, key_head.T, precision=lax.Precision.HIGHEST) * score_scale
        allowed = (key_ids <= group_ids[group_index])[None, :]
        scores = jnp.where(allowed, scores, -1e30)
        peak = jnp.max(scores, axis=-1, keepdims=True)
        weights = jnp.where(allowed, jnp.exp(scores - peak), 0.0)
        total = jnp.sum(weights, axis=-1, keepdims=True)
        output = jnp.dot(weights.astype(jnp.bfloat16), value_head, preferred_element_type=jnp.float32) / total
        return output.astype(jnp.bfloat16)

    group_list = jnp.repeat(jnp.arange(GROUPS, dtype=jnp.int32), HEADS)
    head_list = jnp.tile(jnp.arange(HEADS, dtype=jnp.int32), GROUPS)
    attended = lax.map(one_head, (group_list, head_list))
    attended = attended.reshape(GROUPS, HEADS, GROUP_TOK, HEAD).transpose(0, 2, 1, 3)
    attended = attended.reshape(GROUPS, GROUP_TOK, HEADS * HEAD)
    gates = gate_table[noise_levels]
    done = (attended.astype(jnp.float32) * gates[:, None, :]).astype(jnp.bfloat16)
    return jnp.roll(done, 1, axis=0).reshape(TOKENS, HEADS * HEAD)
```

```python
import functools
import math

import jax
import jax.numpy as jnp
from jax import lax
from jax.experimental import pallas as pl
from jax.experimental.pallas import tpu as pltpu
from jax.sharding import PartitionSpec as P

HEADS = 32
HEAD = 128
GROUPS = 8
TOK = 16
Z = 16
ZLO = 4
SIDE = 4
BLOCK = 256
PART = BLOCK // SIDE
SCALE = math.log2(math.e) / math.sqrt(HEAD)
MESH = pl.DeviceIdType.MESH
V_AFTER = (3, 5, 6, 7)
ORDER = (0, 3, 1, 2)


def kernel(
    levels_ref, ids_ref, q_ref, k_ref, v_ref, gate_ref, out_ref,
    q_in, k_in, v_in, gate, q_all, k_all, v_all, k_cat, v_cat, scores, weights,
    part_out, part_in, stat_out, stat_in, merged, final,
    load_sem, kz_sem, qz_sem, vz_sem, x_sem, y_sem, o_sem, s_sem, f_sem, send_sem,
):
    group, ctx = lax.axis_index("group"), lax.axis_index("ctx")
    zlo, core = group // 2, group % 2
    x, y, zhi = ctx // 16, ctx // 4 % 4, ctx % 4
    z = zhi * ZLO + zlo

    def device(x, y, z, core):
        return (z % ZLO * 2 + core, (x * SIDE + y) * 4 + z // ZLO)

    def column(head):
        return pl.ds(pl.multiple_of(head * HEAD, HEAD), HEAD)

    head = z * 2 + core
    loads = [
        pltpu.make_async_copy(k_ref, k_in, load_sem.at[0]),
        pltpu.make_async_copy(q_ref, q_in, load_sem.at[1]),
        pltpu.make_async_copy(v_ref, v_in, load_sem.at[2]),
        pltpu.make_async_copy(gate_ref.at[:, column(head)], gate, load_sem.at[3]),
    ]
    for load in loads:
        load.start()

    barrier = pltpu.get_barrier_semaphore()

    def greet_z(i, carry):
        pl.semaphore_signal(
            barrier, inc=1, device_id=device(x, y, (z + i // 2) % Z, (core + i) % 2), device_id_type=MESH
        )
        return carry

    lax.fori_loop(1, 2 * Z, greet_z, 0)
    for step in range(1, SIDE):
        pl.semaphore_signal(barrier, inc=1, device_id=device((x + step) % SIDE, y, z, core), device_id_type=MESH)
        pl.semaphore_signal(barrier, inc=1, device_id=device(x, (y + step) % SIDE, z, core), device_id_type=MESH)
    for load in loads:
        load.wait()
    pl.semaphore_wait(barrier, 2 * Z - 1 + 2 * (SIDE - 1))

    own = ((k_in, k_all, kz_sem, 0), (q_in, q_all, qz_sem, 1), (v_in, v_all, vz_sem, 2))
    for source, target, sem, number in own:
        pltpu.make_async_copy(source.at[:, column(head)], target.at[0, 0, 0, core], sem.at[0]).start()

        def send_z(i, carry, source=source, target=target, sem=sem, number=number):
            apart, other = i // 2, i % 2
            to_z, to_core = (z + Z - apart) % Z, (core + other) % 2
            pltpu.make_async_remote_copy(
                src_ref=source.at[:, column(to_z * 2 + to_core)],
                dst_ref=target.at[0, apart // ZLO, apart % ZLO, core],
                send_sem=send_sem.at[number],
                recv_sem=sem.at[apart // ZLO],
                device_id=device(x, y, to_z, to_core),
                device_id_type=MESH,
            ).start()
            return carry

        for chunk in ORDER:
            lax.fori_loop(max(1, 8 * chunk), 8 * chunk + 8, send_z, 0)

    def wait_bytes(ref, sem):
        pltpu.make_async_copy(ref, ref, sem).wait()

    def forward(buffer, chunk, arrived, along_x, send, receive):
        wait_bytes(buffer.at[0, chunk], arrived.at[chunk])
        for step in range(1, SIDE):
            if along_x:
                target = device((x + SIDE - step) % SIDE, y, z, core)
            else:
                target = device(x, (y + SIDE - step) % SIDE, z, core)
            pltpu.make_async_remote_copy(
                src_ref=buffer.at[0, chunk],
                dst_ref=buffer.at[step, chunk],
                send_sem=send,
                recv_sem=receive,
                device_id=target,
                device_id_type=MESH,
            ).start()

    for chunk in ORDER:
        forward(k_all, chunk, kz_sem, True, send_sem.at[3], x_sem.at[0])
    for chunk in ORDER:
        forward(q_all, chunk, qz_sem, False, send_sem.at[4], y_sem)
    wait_bytes(k_all.at[pl.ds(1, SIDE - 1)], x_sem.at[0])
    wait_bytes(q_all.at[pl.ds(1, SIDE - 1)], y_sem)

    def holder(rank):
        found = jnp.int32(0)
        for g in range(GROUPS):
            found = found + jnp.where(ids_ref[g] == rank, jnp.int32(g), jnp.int32(0))
        return found

    ranked = [holder(rank) for rank in range(GROUPS)]
    slots = [((g // 2 - zlo + ZLO) % ZLO, g % 2) for g in ranked]

    def block(buffer, rank):
        near, side = slots[rank]
        return buffer[:, :, near, side].reshape(BLOCK, HEAD)

    for rank in range(GROUPS):
        k_cat[pl.ds(rank * BLOCK, BLOCK), :] = block(k_all, rank)

    for rank in range(GROUPS):
        queries = block(q_all, rank)
        slot = rank % 2
        peak = None
        for other in range(rank + 1):
            keys = k_cat[pl.ds(other * BLOCK, BLOCK), :]
            product = lax.dot_general(
                queries, keys, (((1,), (1,)), ((), ())), preferred_element_type=jnp.float32
            )
            scores[slot, :, pl.ds(other * BLOCK, BLOCK)] = product
            high = jnp.maximum(product[:, :HEAD], product[:, HEAD:])
            peak = high if peak is None else jnp.maximum(peak, high)
        peak = jnp.max(peak, axis=1, keepdims=True)
        stat_out[1, rank] = jnp.broadcast_to(peak, (BLOCK, HEAD))
        for other in range(rank + 1):
            span = pl.ds(other * BLOCK, BLOCK)
            weights[rank, :, span] = jnp.exp2((scores[slot, :, span] - peak) * SCALE).astype(jnp.bfloat16)
        for chunk, after in zip(ORDER, V_AFTER):
            if after == rank:
                forward(v_all, chunk, vz_sem, True, send_sem.at[5], x_sem.at[1])

    wait_bytes(v_all.at[pl.ds(1, SIDE - 1)], x_sem.at[1])
    v_cat[:, HEAD:] = jnp.ones((GROUPS * BLOCK, HEAD), jnp.bfloat16)
    for rank in range(GROUPS):
        v_cat[pl.ds(rank * BLOCK, BLOCK), :HEAD] = block(v_all, rank)

    rows = lax.broadcasted_iota(jnp.int32, (HEAD, HEAD), 0)
    lanes = lax.broadcasted_iota(jnp.int32, (HEAD, HEAD), 1)
    diagonal = rows == lanes
    for rank in range(GROUPS):
        width = (rank + 1) * BLOCK
        product = jnp.dot(
            weights[rank, :, pl.ds(0, width)], v_cat[pl.ds(0, width), :], preferred_element_type=jnp.float32
        )
        total = product[:, HEAD:]
        part_out[rank] = (product[:, :HEAD] / total).astype(jnp.bfloat16).reshape(SIDE, PART, HEAD)
        logs = stat_out[1, rank] * SCALE + jnp.log2(total)
        for half in range(2):
            square = logs[half * HEAD : (half + 1) * HEAD]
            stat_in[0, pl.ds(2 * rank + half, 1), :] = jnp.sum(jnp.where(diagonal, square, 0.0), axis=0, keepdims=True)
        for step in range(1, SIDE):
            pltpu.make_async_remote_copy(
                src_ref=part_out.at[rank, step],
                dst_ref=part_in.at[step - 1, rank],
                send_sem=send_sem.at[6],
                recv_sem=o_sem,
                device_id=device(x, (y + step) % SIDE, z, core),
                device_id_type=MESH,
            ).start()
    for step in range(1, SIDE):
        pltpu.make_async_remote_copy(
            src_ref=stat_in.at[0],
            dst_ref=stat_in.at[step],
            send_sem=send_sem.at[7],
            recv_sem=s_sem,
            device_id=device(x, (y + step) % SIDE, z, core),
            device_id_type=MESH,
        ).start()
    wait_bytes(part_in, o_sem)
    wait_bytes(stat_in.at[pl.ds(1, SIDE - 1)], s_sem)

    part_rows = lax.broadcasted_iota(jnp.int32, (PART, HEAD), 0)
    part_lanes = lax.broadcasted_iota(jnp.int32, (PART, HEAD), 1)
    for rank in range(GROUPS):
        logs = []
        for step in range(SIDE):
            line = stat_in[step, pl.ds(2 * rank + step // 2, 1), :]
            picked = jnp.where(part_lanes == part_rows + step % 2 * PART, line, 0.0)
            logs.append(jnp.sum(picked, axis=1, keepdims=True))
        top = functools.reduce(jnp.maximum, logs)
        shares = [jnp.exp2(log - top) for log in logs]
        whole = functools.reduce(jnp.add, shares)
        value = part_out[rank, 0].astype(jnp.float32) * (shares[0] / whole)
        for step in range(1, SIDE):
            value = value + part_in[step - 1, rank].astype(jnp.float32) * (shares[step] / whole)
        merged[rank] = value.astype(jnp.bfloat16)

    for g in range(GROUPS):
        row = gate[pl.ds(levels_ref[g], 1), :]
        done = merged[ids_ref[g]].astype(jnp.float32) * row
        final[g] = done.astype(jnp.bfloat16).reshape(4, TOK, HEAD)

    def place(i):
        to_z, to_core = (z + i // 2) % Z, (core + i) % 2
        from_group = (to_z % ZLO * 2 + to_core + GROUPS - 1) % GROUPS
        from_z = to_z // ZLO * ZLO + from_group // 2
        return final.at[from_group, (from_z - z + Z) % Z // ZLO], device(x, y, to_z, to_core)

    tile, _ = place(0)
    pltpu.make_async_copy(tile, out_ref.at[:, column(head)], f_sem).start()

    def send_back(i, carry):
        tile, target = place(i)
        pltpu.make_async_remote_copy(
            src_ref=tile,
            dst_ref=out_ref.at[:, column(head)],
            send_sem=send_sem.at[8],
            recv_sem=f_sem,
            device_id=target,
            device_id_type=MESH,
        ).start()
        return carry

    lax.fori_loop(1, 2 * Z, send_back, 0)
    for number, source in enumerate((k_in, q_in, v_in)):
        wait_bytes(source.at[:, pl.ds(0, (2 * Z - 1) * HEAD)], send_sem.at[number])
    wait_bytes(k_all.at[pl.ds(1, SIDE - 1)], send_sem.at[3])
    wait_bytes(q_all.at[pl.ds(1, SIDE - 1)], send_sem.at[4])
    wait_bytes(v_all.at[pl.ds(1, SIDE - 1)], send_sem.at[5])
    wait_bytes(part_in, send_sem.at[6])
    wait_bytes(stat_in.at[pl.ds(1, SIDE - 1)], send_sem.at[7])
    wait_bytes(k_in.at[:, pl.ds(0, (2 * Z - 1) * HEAD)], send_sem.at[8])
    wait_bytes(out_ref, f_sem)


def local(queries, key_states, value_states, gate_table, noise_levels, group_ids):
    bf16, f32 = jnp.bfloat16, jnp.float32
    held = (SIDE, 4, ZLO, 2, TOK, HEAD)
    every = GROUPS * BLOCK
    return pl.pallas_call(
        kernel,
        out_shape=jax.ShapeDtypeStruct((TOK, HEADS * HEAD), bf16),
        in_specs=[pl.BlockSpec(memory_space=pltpu.SMEM)] * 2 + [pl.BlockSpec(memory_space=pl.ANY)] * 4,
        out_specs=pl.BlockSpec(memory_space=pltpu.VMEM),
        scratch_shapes=[
            pltpu.VMEM((TOK, HEADS * HEAD), bf16),
            pltpu.VMEM((TOK, HEADS * HEAD), bf16),
            pltpu.VMEM((TOK, HEADS * HEAD), bf16),
            pltpu.VMEM((32, HEAD), f32),
            pltpu.VMEM(held, bf16),
            pltpu.VMEM(held, bf16),
            pltpu.VMEM(held, bf16),
            pltpu.VMEM((every, HEAD), bf16),
            pltpu.VMEM((every, 2 * HEAD), bf16),
            pltpu.VMEM((2, BLOCK, every), f32),
            pltpu.VMEM((GROUPS, BLOCK, every), bf16),
            pltpu.VMEM((GROUPS, SIDE, PART, HEAD), bf16),
            pltpu.VMEM((SIDE - 1, GROUPS, PART, HEAD), bf16),
            pltpu.VMEM((2, GROUPS, BLOCK, HEAD), f32),
            pltpu.VMEM((SIDE, 2 * GROUPS, HEAD), f32),
            pltpu.VMEM((GROUPS, PART, HEAD), bf16),
            pltpu.VMEM((GROUPS, 4, TOK, HEAD), bf16),
            pltpu.SemaphoreType.DMA((4,)),
            pltpu.SemaphoreType.DMA((4,)),
            pltpu.SemaphoreType.DMA((4,)),
            pltpu.SemaphoreType.DMA((4,)),
            pltpu.SemaphoreType.DMA((2,)),
            pltpu.SemaphoreType.DMA,
            pltpu.SemaphoreType.DMA,
            pltpu.SemaphoreType.DMA,
            pltpu.SemaphoreType.DMA,
            pltpu.SemaphoreType.DMA((9,)),
        ],
        compiler_params=pltpu.CompilerParams(
            collective_id=0, has_side_effects=True, vmem_limit_bytes=40 * 2**20
        ),
    )(noise_levels, group_ids, queries, key_states, value_states, gate_table)


def solution(mesh):
    placed = (
        P(("group", "ctx"), None),
        P(("group", "ctx"), None),
        P(("group", "ctx"), None),
        P(),
        P(),
        P(),
    )
    return jax.shard_map(
        local, mesh=mesh, in_specs=placed, out_specs=P(("group", "ctx"), None), check_vma=False
    )
```

```python
import functools
import math

import jax
import jax.numpy as jnp
from jax import lax
from jax.experimental import pallas as pl
from jax.experimental.pallas import tpu as pltpu
from jax.sharding import PartitionSpec as P

HEADS = 32
HEAD = 128
GROUPS = 8
TOK = 16
Z = 16
ZLO = 4
SQUARE = 4
PARTS = 4
FAR, NEAR = 0, 1
ROWS = SQUARE * TOK
BLOCK = PARTS * ROWS
SCALE = math.log2(math.e) / math.sqrt(HEAD)
MESH = pl.DeviceIdType.MESH


def kernel(
    levels_ref, ids_ref, q_ref, k_ref, v_ref, gate_ref, out_ref,
    q_in, k_in, v_in, gate, q_0, q_1, q_2, q_3, k_all, v_all, q_cat, k_cat, v_cat, scores, weights, summed,
    part_out, part_in, stats, merged, final,
    load_sem, kz_sem, qz_sem, vz_sem, kf_sem, qf_sem, vf_sem, o_sem, s_sem, f_sem, send_sem,
):
    group, ctx = lax.axis_index("group"), lax.axis_index("ctx")
    zlo, core = lax.div(group, 2), lax.rem(group, 2)
    x, y, zhi = lax.div(ctx, 16), lax.rem(lax.div(ctx, 4), 4), lax.rem(ctx, 4)
    z = zhi * ZLO + zlo

    def device(to_x, to_y, to_z, to_core):
        return (lax.rem(to_z, ZLO) * 2 + to_core, (to_x * 4 + to_y) * 4 + lax.div(to_z, ZLO))

    def column(head):
        return pl.ds(pl.multiple_of(head * HEAD, HEAD), HEAD)

    x_even, y_even = x + 1 - 2 * lax.rem(x, 2), y + 1 - 2 * lax.rem(y, 2)
    x_odd, y_odd = lax.rem(x + 3 + 2 * lax.rem(x, 2), 4), lax.rem(y + 3 + 2 * lax.rem(y, 2), 4)
    aligned = [device(x, y, z, core), device(x_even, y, z, core), device(x, y_even, z, core), device(x_even, y_even, z, core)]
    shifted = [device(x, y, z, core), device(x_odd, y, z, core), device(x, y_odd, z, core)]

    head = z * 2 + core
    loads = [
        pltpu.make_async_copy(k_ref, k_in, load_sem.at[0]),
        pltpu.make_async_copy(v_ref, v_in, load_sem.at[1]),
        pltpu.make_async_copy(q_ref, q_in, load_sem.at[2]),
        pltpu.make_async_copy(gate_ref.at[:, column(head)], gate, load_sem.at[3]),
    ]
    for load in loads:
        load.start()

    barrier = pltpu.get_barrier_semaphore()
    for peer in aligned[1:] + shifted[1:3]:
        pl.semaphore_signal(barrier, inc=1, device_id=peer, device_id_type=MESH)

    def greet(i, carry):
        target = device(x, y, lax.rem(z + lax.div(i, 2), Z), lax.rem(core + i, 2))
        pl.semaphore_signal(barrier, inc=1, device_id=target, device_id_type=MESH)
        return carry

    lax.fori_loop(1, 2 * Z, greet, 0)
    for load in loads:
        load.wait()
    pl.semaphore_wait(barrier, 2 * Z - 1 + 5)

    def wait_bytes(ref, sem):
        pltpu.make_async_copy(ref, ref, sem).wait()

    sent = []
    q_parts = (q_0, q_1, q_2, q_3)

    def distance(part, place):
        odd = lax.rem(place + part, 2)
        return place + (8 - 4 * odd if part < 2 else 4 * odd - 4)

    def spread(source, tile, arrived, number, part):
        def send(i, carry):
            place, other = lax.div(i, 2), lax.rem(i, 2)
            to_z, to_core = lax.rem(z + Z - distance(part, place), Z), lax.rem(core + other, 2)
            pltpu.make_async_remote_copy(
                src_ref=source.at[:, column(to_z * 2 + to_core)],
                dst_ref=tile(place),
                send_sem=send_sem.at[number],
                recv_sem=arrived,
                device_id=device(x, y, to_z, to_core),
                device_id_type=MESH,
            ).start()
            return carry

        if part == PARTS - 1:
            pltpu.make_async_copy(source.at[:, column(head)], tile(0), arrived).start()
            lax.fori_loop(1, 8, send, 0)
        else:
            lax.fori_loop(0, 8, send, 0)

    for part in range(PARTS):
        spread(k_in, lambda place: k_all.at[0, part, place, core], kz_sem.at[part // 2], 0, part)
    for part in range(PARTS):
        spread(v_in, lambda place: v_all.at[0, part, place, core], vz_sem.at[part // 2], 1, part)
    for part in range(PARTS):
        spread(q_in, lambda place: q_parts[part].at[0, place, core], qz_sem.at[part], 2, part)
    sent += [(source.at[:, pl.ds(0, (2 * Z - 1) * HEAD)], number) for number, source in enumerate((k_in, v_in, q_in))]

    halves = (pl.ds(0, 2), pl.ds(2, 2))
    others = pl.ds(1, SQUARE - 1)

    def pass_on(source, target_ref, target, number, receive):
        pltpu.make_async_remote_copy(
            src_ref=source,
            dst_ref=target_ref,
            send_sem=send_sem.at[number],
            recv_sem=receive,
            device_id=target,
            device_id_type=MESH,
        ).start()

    def pass_near(buffer, arrived, number, receive):
        for half, span in enumerate(halves):
            wait_bytes(buffer.at[0, span], arrived.at[half])
            for step in (1, 2):
                early = half == step - 1
                pass_on(
                    buffer.at[0, span], buffer.at[step, span], shifted[step], number, receive.at[half if early else 2]
                )

    def pass_across(buffer, number, receive):
        for half, span in enumerate(halves):
            wait_bytes(buffer.at[half + 1, span], receive.at[half])
            pass_on(buffer.at[half + 1, span], buffer.at[3, span], shifted[2 - half], number, receive.at[2])

    def pass_queries(part):
        queries = q_parts[part]
        wait_bytes(queries.at[0], qz_sem.at[part])
        for step in range(1, SQUARE):
            pass_on(queries.at[0], queries.at[step], aligned[step], 5, qf_sem.at[part])

    pass_near(k_all, kz_sem, 3, kf_sem)
    pass_across(k_all, 3, kf_sem)
    pass_near(v_all, vz_sem, 4, vf_sem)
    pass_queries(0)
    pass_across(v_all, 4, vf_sem)
    pass_queries(1)
    pass_queries(2)

    def holder(rank):
        found = jnp.int32(0)
        for g in range(GROUPS):
            found = found + jnp.where(ids_ref[g] == rank, jnp.int32(g), jnp.int32(0))
        return found

    ranked = [holder(rank) for rank in range(GROUPS)]
    places = [(lax.rem(lax.div(g, 2) - zlo + ZLO, ZLO), lax.rem(g, 2)) for g in ranked]

    wait_bytes(k_all.at[pl.ds(1, 2)], kf_sem.at[2])
    for rank, (near, side) in enumerate(places):
        k_cat[pl.ds(rank * BLOCK, BLOCK), :] = k_all[:, :, near, side].reshape(BLOCK, HEAD)
    v_cat[:, HEAD:] = jnp.ones((GROUPS * BLOCK, HEAD), jnp.bfloat16)
    pass_queries(3)
    wait_bytes(v_all.at[pl.ds(1, 2)], vf_sem.at[2])
    for rank, (near, side) in enumerate(places):
        v_cat[pl.ds(rank * BLOCK, BLOCK), :HEAD] = v_all[:, :, near, side].reshape(BLOCK, HEAD)
    sent += [(k_all.at[others], 3), (v_all.at[others], 4), (k_all.at[others], 5)]

    rows = lax.broadcasted_iota(jnp.int32, (ROWS, HEAD), 0)
    lanes = lax.broadcasted_iota(jnp.int32, (ROWS, HEAD), 1)
    diagonal = rows == lanes

    def attend(part):
        wait_bytes(q_parts[part].at[others], qf_sem.at[part])
        for rank, (near, side) in enumerate(places):
            q_cat[pl.ds(rank * ROWS, ROWS), :] = q_parts[part][:, near, side].reshape(ROWS, HEAD)
        for block in range(GROUPS):
            below = pl.ds(block * ROWS, (GROUPS - block) * ROWS)
            span = pl.ds(block * BLOCK, BLOCK)
            scores[below, span] = lax.dot_general(
                q_cat[below, :], k_cat[span, :], (((1,), (1,)), ((), ())), preferred_element_type=jnp.float32
            )
        peaks = []
        for rank in range(GROUPS):
            own = pl.ds(rank * ROWS, ROWS)
            strips = [scores[own, pl.ds(i * HEAD, HEAD)] for i in range((rank + 1) * BLOCK // HEAD)]
            peak = jnp.max(functools.reduce(jnp.maximum, strips), axis=1, keepdims=True)
            peaks.append(peak)
            for block in range(rank + 1):
                span = pl.ds(block * BLOCK, BLOCK)
                weights[own, span] = jnp.exp2((scores[own, span] - peak) * SCALE).astype(jnp.bfloat16)
        for block in range(GROUPS):
            below = pl.ds(block * ROWS, (GROUPS - block) * ROWS)
            span = pl.ds(block * BLOCK, BLOCK)
            product = jnp.dot(weights[below, span], v_cat[span, :], preferred_element_type=jnp.float32)
            if block == 0:
                summed[below, :] = product
            else:
                summed[below, :] += product
        for rank in range(GROUPS):
            own = pl.ds(rank * ROWS, ROWS)
            total = summed[own, HEAD:]
            part_out[part, :, rank] = (summed[own, :HEAD] / total).astype(jnp.bfloat16).reshape(SQUARE, TOK, HEAD)
            logs = peaks[rank] * SCALE + jnp.log2(total)
            stats[part, 0, pl.ds(rank, 1), :] = jnp.sum(jnp.where(diagonal, logs, 0.0), axis=0, keepdims=True)
        for step in range(1, SQUARE):
            pltpu.make_async_remote_copy(
                src_ref=part_out.at[part, step],
                dst_ref=part_in.at[part, step - 1],
                send_sem=send_sem.at[6],
                recv_sem=o_sem.at[part],
                device_id=aligned[step],
                device_id_type=MESH,
            ).start()
            pltpu.make_async_remote_copy(
                src_ref=stats.at[part, 0],
                dst_ref=stats.at[part, step],
                send_sem=send_sem.at[7],
                recv_sem=s_sem.at[part],
                device_id=aligned[step],
                device_id_type=MESH,
            ).start()

    own_rows = lax.broadcasted_iota(jnp.int32, (TOK, HEAD), 0)
    own_lanes = lax.broadcasted_iota(jnp.int32, (TOK, HEAD), 1)

    def merge(part):
        wait_bytes(part_in.at[part], o_sem.at[part])
        wait_bytes(stats.at[part, others], s_sem.at[part])
        for rank in range(GROUPS):
            logs = []
            for step in range(SQUARE):
                line = stats[part, step, pl.ds(rank, 1), :]
                picked = jnp.where(own_lanes == own_rows + step * TOK, line, 0.0)
                logs.append(jnp.sum(picked, axis=1, keepdims=True))
            top = functools.reduce(jnp.maximum, logs)
            shares = [jnp.exp2(log - top) for log in logs]
            whole = functools.reduce(jnp.add, shares)
            value = part_out[part, 0, rank].astype(jnp.float32) * (shares[0] / whole)
            for step in range(1, SQUARE):
                value = value + part_in[part, step - 1, rank].astype(jnp.float32) * (shares[step] / whole)
            merged[part, rank] = value.astype(jnp.bfloat16)
        for g in range(GROUPS):
            row = gate[pl.ds(levels_ref[g], 1), :]
            done = merged[part, ids_ref[g]].astype(jnp.float32) * row
            final[part, g] = done.astype(jnp.bfloat16)

        def send(i, carry):
            place, side = lax.div(i, 2), lax.rem(i, 2)
            from_z = lax.rem(z + Z + distance(part, place), Z)
            from_group = lax.rem(from_z, ZLO) * 2 + side
            to_group = lax.rem(from_group + 1, GROUPS)
            to_z, to_core = lax.div(from_z, ZLO) * ZLO + lax.div(to_group, 2), lax.rem(to_group, 2)
            away = jnp.logical_or(to_z != z, to_core != core)

            @pl.when(away)
            def _():
                pltpu.make_async_remote_copy(
                    src_ref=final.at[part, from_group],
                    dst_ref=out_ref.at[:, column(head)],
                    send_sem=send_sem.at[8],
                    recv_sem=f_sem,
                    device_id=device(x, y, to_z, to_core),
                    device_id_type=MESH,
                ).start()

            @pl.when(jnp.logical_not(away))
            def _():
                pltpu.make_async_copy(final.at[part, from_group], out_ref.at[:, column(head)], f_sem).start()

            return carry

        lax.fori_loop(0, 8, send, 0)

    for part in range(PARTS):
        attend(part)
    sent += [(part_in, 6), (stats.at[:, others], 7), (k_in.at[:, pl.ds(0, (2 * Z - 1) * HEAD)], 8)]
    for part in range(PARTS):
        merge(part)
    for ref, number in sent:
        wait_bytes(ref, send_sem.at[number])
    wait_bytes(out_ref, f_sem)


def local(queries, key_states, value_states, gate_table, noise_levels, group_ids):
    bf16, f32 = jnp.bfloat16, jnp.float32
    held = (SQUARE, PARTS, ZLO, 2, TOK, HEAD)
    every = GROUPS * BLOCK
    return pl.pallas_call(
        kernel,
        out_shape=jax.ShapeDtypeStruct((TOK, HEADS * HEAD), bf16),
        in_specs=[pl.BlockSpec(memory_space=pltpu.SMEM)] * 2 + [pl.BlockSpec(memory_space=pl.ANY)] * 4,
        out_specs=pl.BlockSpec(memory_space=pltpu.VMEM),
        scratch_shapes=[
            pltpu.VMEM((TOK, HEADS * HEAD), bf16),
            pltpu.VMEM((TOK, HEADS * HEAD), bf16),
            pltpu.VMEM((TOK, HEADS * HEAD), bf16),
            pltpu.VMEM((32, HEAD), f32),
            *[pltpu.VMEM((SQUARE, ZLO, 2, TOK, HEAD), bf16)] * PARTS,
            pltpu.VMEM(held, bf16),
            pltpu.VMEM(held, bf16),
            pltpu.VMEM((GROUPS * ROWS, HEAD), bf16),
            pltpu.VMEM((every, HEAD), bf16),
            pltpu.VMEM((every, 2 * HEAD), bf16),
            pltpu.VMEM((GROUPS * ROWS, every), f32),
            pltpu.VMEM((GROUPS * ROWS, every), bf16),
            pltpu.VMEM((GROUPS * ROWS, 2 * HEAD), f32),
            pltpu.VMEM((PARTS, SQUARE, GROUPS, TOK, HEAD), bf16),
            pltpu.VMEM((PARTS, SQUARE - 1, GROUPS, TOK, HEAD), bf16),
            pltpu.VMEM((PARTS, SQUARE, GROUPS, HEAD), f32),
            pltpu.VMEM((PARTS, GROUPS, TOK, HEAD), bf16),
            pltpu.VMEM((PARTS, GROUPS, TOK, HEAD), bf16),
            pltpu.SemaphoreType.DMA((4,)),
            pltpu.SemaphoreType.DMA((2,)),
            pltpu.SemaphoreType.DMA((PARTS,)),
            pltpu.SemaphoreType.DMA((2,)),
            pltpu.SemaphoreType.DMA((3,)),
            pltpu.SemaphoreType.DMA((PARTS,)),
            pltpu.SemaphoreType.DMA((3,)),
            pltpu.SemaphoreType.DMA((PARTS,)),
            pltpu.SemaphoreType.DMA((PARTS,)),
            pltpu.SemaphoreType.DMA,
            pltpu.SemaphoreType.DMA((9,)),
        ],
        compiler_params=pltpu.CompilerParams(
            collective_id=0, has_side_effects=True, vmem_limit_bytes=56 * 2**20
        ),
    )(noise_levels, group_ids, queries, key_states, value_states, gate_table)


def solution(mesh):
    placed = (
        P(("group", "ctx"), None),
        P(("group", "ctx"), None),
        P(("group", "ctx"), None),
        P(),
        P(),
        P(),
    )
    return jax.shard_map(
        local, mesh=mesh, in_specs=placed, out_specs=P(("group", "ctx"), None), check_vma=False
    )
```

```python
import functools
import math

import jax
import jax.numpy as jnp
from jax import lax
from jax.experimental import pallas as pl
from jax.experimental.pallas import tpu as pltpu
from jax.sharding import PartitionSpec as P

HEADS = 32
HEAD = 128
GROUPS = 8
TOK = 16
Z = 16
ZLO = 4
SQUARE = 4
PARTS = 4
ROWS = SQUARE * TOK
BLOCK = PARTS * ROWS
SCALE = math.log2(math.e) / math.sqrt(HEAD)
MESH = pl.DeviceIdType.MESH


def kernel(
    levels_ref, ids_ref, q_ref, k_ref, v_ref, gate_ref, out_ref,
    q_in, k_in, v_in, gate, q_0, q_1, q_2, q_3, k_all, v_all, q_cat, k_cat, v_cat, scores, weights, summed,
    part_out, part_in, stats, merged, final,
    load_sem, kz_sem, qz_sem, vz_sem, kf_sem, qf_sem, vf_sem, o_sem, s_sem, f_sem, send_sem,
):
    group, ctx = lax.axis_index("group"), lax.axis_index("ctx")
    zlo, core = lax.div(group, 2), lax.rem(group, 2)
    x, y, zhi = lax.div(ctx, 16), lax.rem(lax.div(ctx, 4), 4), lax.rem(ctx, 4)
    z = zhi * ZLO + zlo

    def device(to_x, to_y, to_z, to_core):
        return (lax.rem(to_z, ZLO) * 2 + to_core, (to_x * 4 + to_y) * 4 + lax.div(to_z, ZLO))

    def column(head):
        return pl.ds(pl.multiple_of(head * HEAD, HEAD), HEAD)

    def square(shift):
        def partner(position):
            moved = lax.rem(position + shift, 4)
            return lax.rem(moved + 1 - 2 * lax.rem(moved, 2) + 4 - shift, 4)

        to_x, to_y = partner(x), partner(y)
        return [device(to_x, y, z, core), device(x, to_y, z, core), device(to_x, to_y, z, core)]

    key_square, query_square = square(1 - core), square(core)

    head = z * 2 + core
    loads = [
        pltpu.make_async_copy(k_ref, k_in, load_sem.at[0]),
        pltpu.make_async_copy(v_ref, v_in, load_sem.at[1]),
        pltpu.make_async_copy(q_ref, q_in, load_sem.at[2]),
        pltpu.make_async_copy(gate_ref.at[:, column(head)], gate, load_sem.at[3]),
    ]
    for load in loads:
        load.start()

    barrier = pltpu.get_barrier_semaphore()
    for peer in query_square + key_square:
        pl.semaphore_signal(barrier, inc=1, device_id=peer, device_id_type=MESH)

    def greet(i, carry):
        target = device(x, y, lax.rem(z + lax.div(i, 2), Z), lax.rem(core + i, 2))
        pl.semaphore_signal(barrier, inc=1, device_id=target, device_id_type=MESH)
        return carry

    lax.fori_loop(1, 2 * Z, greet, 0)
    for load in loads:
        load.wait()
    pl.semaphore_wait(barrier, 2 * Z - 1 + 2 * (SQUARE - 1))

    def wait_bytes(ref, sem):
        pltpu.make_async_copy(ref, ref, sem).wait()

    sent = []
    q_parts = (q_0, q_1, q_2, q_3)

    def distance(part, place):
        odd = lax.rem(place + part, 2)
        return place + (8 - 4 * odd if part < 2 else 4 * odd - 4)

    def spread(source, tile, arrived, number, part):
        def send(i, carry):
            place, other = lax.div(i, 2), lax.rem(i, 2)
            to_z, to_core = lax.rem(z + Z - distance(part, place), Z), lax.rem(core + other, 2)
            pltpu.make_async_remote_copy(
                src_ref=source.at[:, column(to_z * 2 + to_core)],
                dst_ref=tile(place),
                send_sem=send_sem.at[number],
                recv_sem=arrived,
                device_id=device(x, y, to_z, to_core),
                device_id_type=MESH,
            ).start()
            return carry

        if part == PARTS - 1:
            pltpu.make_async_copy(source.at[:, column(head)], tile(0), arrived).start()
            lax.fori_loop(1, 8, send, 0)
        else:
            lax.fori_loop(0, 8, send, 0)

    for part in (1, 0):
        spread(k_in, lambda place: k_all.at[0, part, place, core], kz_sem.at[part], 0, part)
    for part in (3, 2):
        spread(k_in, lambda place: k_all.at[0, part, place, core], kz_sem.at[part], 0, part)
    for part in (1, 0):
        spread(v_in, lambda place: v_all.at[0, part, place, core], vz_sem.at[part], 1, part)
    for part in (3, 2):
        spread(v_in, lambda place: v_all.at[0, part, place, core], vz_sem.at[part], 1, part)
    def spread_queries(parts):
        for part in parts:
            spread(q_in, lambda place: q_parts[part].at[0, place, core], qz_sem.at[part], 2, part)

    sent += [(source.at[:, pl.ds(0, (2 * Z - 1) * HEAD)], number) for number, source in enumerate((k_in, v_in, q_in))]

    others = pl.ds(1, SQUARE - 1)

    def pass_on(source, target_ref, target, number, receive):
        pltpu.make_async_remote_copy(
            src_ref=source,
            dst_ref=target_ref,
            send_sem=send_sem.at[number],
            recv_sem=receive,
            device_id=target,
            device_id_type=MESH,
        ).start()

    def pass_part(buffer, part, arrived, number, receive):
        wait_bytes(buffer.at[0, part], arrived.at[part])
        for step in range(1, SQUARE):
            pass_on(buffer.at[0, part], buffer.at[step, part], key_square[step - 1], number, receive)

    def pass_queries(part):
        queries = q_parts[part]
        wait_bytes(queries.at[0], qz_sem.at[part])
        for step in range(1, SQUARE):
            pass_on(queries.at[0], queries.at[step], query_square[step - 1], 5, qf_sem.at[part])

    for part in (1, 0):
        pass_part(k_all, part, kz_sem, 3, kf_sem)
    for part in (3, 2):
        pass_part(k_all, part, kz_sem, 3, kf_sem)
    spread_queries((0, 1))
    for part in (1, 0):
        pass_part(v_all, part, vz_sem, 4, vf_sem)
    for part in (3, 2):
        pass_part(v_all, part, vz_sem, 4, vf_sem)
    spread_queries((2, 3))
    for part in range(PARTS - 1):
        pass_queries(part)

    def holder(rank):
        found = jnp.int32(0)
        for g in range(GROUPS):
            found = found + jnp.where(ids_ref[g] == rank, jnp.int32(g), jnp.int32(0))
        return found

    ranked = [holder(rank) for rank in range(GROUPS)]
    places = [(lax.rem(lax.div(g, 2) - zlo + ZLO, ZLO), lax.rem(g, 2)) for g in ranked]

    wait_bytes(k_all.at[others], kf_sem)
    for rank, (near, side) in enumerate(places):
        k_cat[pl.ds(rank * BLOCK, BLOCK), :] = k_all[:, :, near, side].reshape(BLOCK, HEAD)
    pass_queries(PARTS - 1)
    sent += [(k_all.at[others], 3), (v_all.at[others], 4), (k_all.at[others], 5)]

    rows = lax.broadcasted_iota(jnp.int32, (ROWS, HEAD), 0)
    lanes = lax.broadcasted_iota(jnp.int32, (ROWS, HEAD), 1)
    diagonal = rows == lanes

    def score(part):
        wait_bytes(q_parts[part].at[others], qf_sem.at[part])
        for rank, (near, side) in enumerate(places):
            q_cat[pl.ds(rank * ROWS, ROWS), :] = q_parts[part][:, near, side].reshape(ROWS, HEAD)
        for block in range(GROUPS):
            below = pl.ds(block * ROWS, (GROUPS - block) * ROWS)
            span = pl.ds(block * BLOCK, BLOCK)
            scores[below, span] = lax.dot_general(
                q_cat[below, :], k_cat[span, :], (((1,), (1,)), ((), ())), preferred_element_type=jnp.float32
            )
        peaks = []
        for rank in range(GROUPS):
            own = pl.ds(rank * ROWS, ROWS)
            strips = [scores[own, pl.ds(i * HEAD, HEAD)] for i in range((rank + 1) * BLOCK // HEAD)]
            peak = jnp.max(functools.reduce(jnp.maximum, strips), axis=1, keepdims=True)
            peaks.append(peak)
            for block in range(rank + 1):
                span = pl.ds(block * BLOCK, BLOCK)
                weights[own, span] = jnp.exp2((scores[own, span] - peak) * SCALE).astype(jnp.bfloat16)
        return peaks

    def attend(part, peaks):
        for block in range(GROUPS):
            below = pl.ds(block * ROWS, (GROUPS - block) * ROWS)
            span = pl.ds(block * BLOCK, BLOCK)
            product = jnp.dot(weights[below, span], v_cat[span, :], preferred_element_type=jnp.float32)
            if block == 0:
                summed[below, :] = product
            else:
                summed[below, :] += product
        for rank in range(GROUPS):
            own = pl.ds(rank * ROWS, ROWS)
            total = summed[own, HEAD:]
            part_out[part, :, rank] = (summed[own, :HEAD] / total).astype(jnp.bfloat16).reshape(SQUARE, TOK, HEAD)
            logs = peaks[rank] * SCALE + jnp.log2(total)
            stats[part, 0, pl.ds(rank, 1), :] = jnp.sum(jnp.where(diagonal, logs, 0.0), axis=0, keepdims=True)
        for step in range(1, SQUARE):
            pltpu.make_async_remote_copy(
                src_ref=part_out.at[part, step],
                dst_ref=part_in.at[part, step - 1],
                send_sem=send_sem.at[6],
                recv_sem=o_sem.at[part],
                device_id=query_square[step - 1],
                device_id_type=MESH,
            ).start()
            pltpu.make_async_remote_copy(
                src_ref=stats.at[part, 0],
                dst_ref=stats.at[part, step],
                send_sem=send_sem.at[7],
                recv_sem=s_sem.at[part],
                device_id=query_square[step - 1],
                device_id_type=MESH,
            ).start()

    own_rows = lax.broadcasted_iota(jnp.int32, (TOK, HEAD), 0)
    own_lanes = lax.broadcasted_iota(jnp.int32, (TOK, HEAD), 1)

    def merge(part):
        wait_bytes(part_in.at[part], o_sem.at[part])
        wait_bytes(stats.at[part, others], s_sem.at[part])
        for rank in range(GROUPS):
            logs = []
            for step in range(SQUARE):
                line = stats[part, step, pl.ds(rank, 1), :]
                picked = jnp.where(own_lanes == own_rows + step * TOK, line, 0.0)
                logs.append(jnp.sum(picked, axis=1, keepdims=True))
            top = functools.reduce(jnp.maximum, logs)
            shares = [jnp.exp2(log - top) for log in logs]
            whole = functools.reduce(jnp.add, shares)
            value = part_out[part, 0, rank].astype(jnp.float32) * (shares[0] / whole)
            for step in range(1, SQUARE):
                value = value + part_in[part, step - 1, rank].astype(jnp.float32) * (shares[step] / whole)
            merged[part, rank] = value.astype(jnp.bfloat16)
        for g in range(GROUPS):
            row = gate[pl.ds(levels_ref[g], 1), :]
            done = merged[part, ids_ref[g]].astype(jnp.float32) * row
            final[part, g] = done.astype(jnp.bfloat16)

    def give(part, lower):
        def send(i, carry):
            place, side = lax.div(i, 2), lax.rem(i, 2)
            from_z = lax.rem(z + Z + distance(part, place), Z)
            from_group = lax.rem(from_z, ZLO) * 2 + side
            to_group = lax.rem(from_group + 1, GROUPS)
            to_z, to_core = lax.div(from_z, ZLO) * ZLO + lax.div(to_group, 2), lax.rem(to_group, 2)
            away = jnp.logical_or(to_z != z, to_core != core)
            now = to_z < Z // 2 if lower else to_z >= Z // 2

            @pl.when(jnp.logical_and(now, away))
            def _():
                pltpu.make_async_remote_copy(
                    src_ref=final.at[part, from_group],
                    dst_ref=out_ref.at[:, column(head)],
                    send_sem=send_sem.at[8],
                    recv_sem=f_sem,
                    device_id=device(x, y, to_z, to_core),
                    device_id_type=MESH,
                ).start()

            @pl.when(jnp.logical_and(now, jnp.logical_not(away)))
            def _():
                pltpu.make_async_copy(final.at[part, from_group], out_ref.at[:, column(head)], f_sem).start()

            return carry

        lax.fori_loop(0, 8, send, 0)

    peaks = score(0)
    v_cat[:, HEAD:] = jnp.ones((GROUPS * BLOCK, HEAD), jnp.bfloat16)
    wait_bytes(v_all.at[others], vf_sem)
    for rank, (near, side) in enumerate(places):
        v_cat[pl.ds(rank * BLOCK, BLOCK), :HEAD] = v_all[:, :, near, side].reshape(BLOCK, HEAD)
    attend(0, peaks)
    attend(1, score(1))
    attend(2, score(2))
    merge(0)
    give(0, True)
    attend(3, score(3))
    sent += [(part_in, 6), (stats.at[:, others], 7), (k_in.at[:, pl.ds(0, (2 * Z - 1) * HEAD)], 8)]
    for part in range(1, PARTS):
        merge(part)
        give(part, True)
    for part in range(PARTS):
        give(part, False)
    for ref, number in sent:
        wait_bytes(ref, send_sem.at[number])
    wait_bytes(out_ref, f_sem)


def local(queries, key_states, value_states, gate_table, noise_levels, group_ids):
    bf16, f32 = jnp.bfloat16, jnp.float32
    held = (SQUARE, PARTS, ZLO, 2, TOK, HEAD)
    every = GROUPS * BLOCK
    return pl.pallas_call(
        kernel,
        out_shape=jax.ShapeDtypeStruct((TOK, HEADS * HEAD), bf16),
        in_specs=[pl.BlockSpec(memory_space=pltpu.SMEM)] * 2 + [pl.BlockSpec(memory_space=pl.ANY)] * 4,
        out_specs=pl.BlockSpec(memory_space=pltpu.VMEM),
        scratch_shapes=[
            pltpu.VMEM((TOK, HEADS * HEAD), bf16),
            pltpu.VMEM((TOK, HEADS * HEAD), bf16),
            pltpu.VMEM((TOK, HEADS * HEAD), bf16),
            pltpu.VMEM((32, HEAD), f32),
            *[pltpu.VMEM((SQUARE, ZLO, 2, TOK, HEAD), bf16)] * PARTS,
            pltpu.VMEM(held, bf16),
            pltpu.VMEM(held, bf16),
            pltpu.VMEM((GROUPS * ROWS, HEAD), bf16),
            pltpu.VMEM((every, HEAD), bf16),
            pltpu.VMEM((every, 2 * HEAD), bf16),
            pltpu.VMEM((GROUPS * ROWS, every), f32),
            pltpu.VMEM((GROUPS * ROWS, every), bf16),
            pltpu.VMEM((GROUPS * ROWS, 2 * HEAD), f32),
            pltpu.VMEM((PARTS, SQUARE, GROUPS, TOK, HEAD), bf16),
            pltpu.VMEM((PARTS, SQUARE - 1, GROUPS, TOK, HEAD), bf16),
            pltpu.VMEM((PARTS, SQUARE, GROUPS, HEAD), f32),
            pltpu.VMEM((PARTS, GROUPS, TOK, HEAD), bf16),
            pltpu.VMEM((PARTS, GROUPS, TOK, HEAD), bf16),
            pltpu.SemaphoreType.DMA((4,)),
            pltpu.SemaphoreType.DMA((PARTS,)),
            pltpu.SemaphoreType.DMA((PARTS,)),
            pltpu.SemaphoreType.DMA((PARTS,)),
            pltpu.SemaphoreType.DMA,
            pltpu.SemaphoreType.DMA((PARTS,)),
            pltpu.SemaphoreType.DMA,
            pltpu.SemaphoreType.DMA((PARTS,)),
            pltpu.SemaphoreType.DMA((PARTS,)),
            pltpu.SemaphoreType.DMA,
            pltpu.SemaphoreType.DMA((9,)),
        ],
        compiler_params=pltpu.CompilerParams(
            collective_id=0, has_side_effects=True, vmem_limit_bytes=56 * 2**20
        ),
    )(noise_levels, group_ids, queries, key_states, value_states, gate_table)


def solution(mesh):
    placed = (
        P(("group", "ctx"), None),
        P(("group", "ctx"), None),
        P(("group", "ctx"), None),
        P(),
        P(),
        P(),
    )
    return jax.shard_map(
        local, mesh=mesh, in_specs=placed, out_specs=P(("group", "ctx"), None), check_vma=False
    )
```

```python
import functools
import math

import jax
import jax.numpy as jnp
from jax import lax
from jax.experimental import pallas as pl
from jax.experimental.pallas import tpu as pltpu
from jax.sharding import PartitionSpec as P

HEADS = 32
HEAD = 128
GROUPS = 8
TOK = 16
Z = 16
ZLO = 4
SQUARE = 4
PARTS = 4
ROWS = SQUARE * TOK
BLOCK = PARTS * ROWS
ACROSS_FIRST = (3, 1, 2)
SCALE = math.log2(math.e) / math.sqrt(HEAD)
MESH = pl.DeviceIdType.MESH


def kernel(
    levels_ref, ids_ref, q_ref, k_ref, v_ref, gate_ref, out_ref,
    q_in, k_in, v_in, gate, q_0, q_1, q_2, q_3, k_all, v_all, q_cat, k_cat, v_cat, scores, weights, summed,
    part_out, part_in, stats, merged, final,
    load_sem, kz_sem, qz_sem, vz_sem, kf_sem, qf_sem, vf_sem, o_sem, s_sem, f_sem, send_sem,
):
    group, ctx = lax.axis_index("group"), lax.axis_index("ctx")
    zlo, core = lax.div(group, 2), lax.rem(group, 2)
    x, y, zhi = lax.div(ctx, 16), lax.rem(lax.div(ctx, 4), 4), lax.rem(ctx, 4)
    z = zhi * ZLO + zlo

    def device(to_x, to_y, to_z, to_core):
        return (lax.rem(to_z, ZLO) * 2 + to_core, (to_x * 4 + to_y) * 4 + lax.div(to_z, ZLO))

    def column(head):
        return pl.ds(pl.multiple_of(head * HEAD, HEAD), HEAD)

    def square(shift):
        def partner(position):
            moved = lax.rem(position + shift, 4)
            return lax.rem(moved + 1 - 2 * lax.rem(moved, 2) + 4 - shift, 4)

        to_x, to_y = partner(x), partner(y)
        return [device(to_x, y, z, core), device(x, to_y, z, core), device(to_x, to_y, z, core)]

    key_square, query_square = square(1 - core), square(core)

    head = z * 2 + core
    loads = [
        pltpu.make_async_copy(k_ref, k_in, load_sem.at[0]),
        pltpu.make_async_copy(v_ref, v_in, load_sem.at[1]),
        pltpu.make_async_copy(q_ref, q_in, load_sem.at[2]),
        pltpu.make_async_copy(gate_ref.at[:, column(head)], gate, load_sem.at[3]),
    ]
    for load in loads:
        load.start()

    barrier = pltpu.get_barrier_semaphore()
    for peer in query_square + key_square:
        pl.semaphore_signal(barrier, inc=1, device_id=peer, device_id_type=MESH)

    def greet(i, carry):
        target = device(x, y, lax.rem(z + lax.div(i, 2), Z), lax.rem(core + i, 2))
        pl.semaphore_signal(barrier, inc=1, device_id=target, device_id_type=MESH)
        return carry

    lax.fori_loop(1, 2 * Z, greet, 0)
    for load in loads:
        load.wait()
    pl.semaphore_wait(barrier, 2 * Z - 1 + 2 * (SQUARE - 1))

    def wait_bytes(ref, sem):
        pltpu.make_async_copy(ref, ref, sem).wait()

    sent = []
    q_parts = (q_0, q_1, q_2, q_3)

    def distance(part, place):
        odd = (place + part) % 2
        return place + (8 - 4 * odd if part < 2 else 4 * odd - 4)

    def spread(source, tile, arrived, number, part):
        for place in range(ZLO):
            to_z = lax.rem(z + Z - distance(part, place), Z)
            for to_core in (core, 1 - core):
                if distance(part, place) == 0 and to_core is core:
                    pltpu.make_async_copy(source.at[:, column(head)], tile(place), arrived).start()
                    continue
                pltpu.make_async_remote_copy(
                    src_ref=source.at[:, column(to_z * 2 + to_core)],
                    dst_ref=tile(place),
                    send_sem=send_sem.at[number],
                    recv_sem=arrived,
                    device_id=device(x, y, to_z, to_core),
                    device_id_type=MESH,
                ).start()

    for part in (1, 0):
        spread(k_in, lambda place: k_all.at[0, part, place, core], kz_sem.at[part], 0, part)
    for part in (3, 2):
        spread(k_in, lambda place: k_all.at[0, part, place, core], kz_sem.at[part], 0, part)
    for part in (1, 0):
        spread(v_in, lambda place: v_all.at[0, part, place, core], vz_sem.at[part], 1, part)
    for part in (3, 2):
        spread(v_in, lambda place: v_all.at[0, part, place, core], vz_sem.at[part], 1, part)

    def spread_queries(parts):
        for part in parts:
            spread(q_in, lambda place: q_parts[part].at[0, place, core], qz_sem.at[part], 2, part)

    sent += [(source.at[:, pl.ds(0, (2 * Z - 1) * HEAD)], number) for number, source in enumerate((k_in, v_in, q_in))]

    others = pl.ds(1, SQUARE - 1)

    def pass_on(source, target_ref, target, number, receive):
        pltpu.make_async_remote_copy(
            src_ref=source,
            dst_ref=target_ref,
            send_sem=send_sem.at[number],
            recv_sem=receive,
            device_id=target,
            device_id_type=MESH,
        ).start()

    def pass_part(buffer, part, arrived, number, receive):
        wait_bytes(buffer.at[0, part], arrived.at[part])
        for step in ACROSS_FIRST:
            pass_on(buffer.at[0, part], buffer.at[step, part], key_square[step - 1], number, receive)

    def pass_queries(part):
        queries = q_parts[part]
        wait_bytes(queries.at[0], qz_sem.at[part])
        for step in ACROSS_FIRST:
            pass_on(queries.at[0], queries.at[step], query_square[step - 1], 5, qf_sem.at[part])

    for part in (1, 0):
        pass_part(k_all, part, kz_sem, 3, kf_sem)
    for part in (3, 2):
        pass_part(k_all, part, kz_sem, 3, kf_sem)
    spread_queries((0, 1))
    for part in (1, 0):
        pass_part(v_all, part, vz_sem, 4, vf_sem)
    for part in (3, 2):
        pass_part(v_all, part, vz_sem, 4, vf_sem)
    spread_queries((2, 3))
    for part in range(PARTS - 1):
        pass_queries(part)

    def holder(rank):
        found = jnp.int32(0)
        for g in range(GROUPS):
            found = found + jnp.where(ids_ref[g] == rank, jnp.int32(g), jnp.int32(0))
        return found

    ranked = [holder(rank) for rank in range(GROUPS)]
    places = [(lax.rem(lax.div(g, 2) - zlo + ZLO, ZLO), lax.rem(g, 2)) for g in ranked]

    wait_bytes(k_all.at[others], kf_sem)
    for rank, (near, side) in enumerate(places):
        k_cat[pl.ds(rank * BLOCK, BLOCK), :] = k_all[:, :, near, side].reshape(BLOCK, HEAD)
    pass_queries(PARTS - 1)
    sent += [(k_all.at[others], 3), (v_all.at[others], 4), (k_all.at[others], 5)]

    rows = lax.broadcasted_iota(jnp.int32, (ROWS, HEAD), 0)
    lanes = lax.broadcasted_iota(jnp.int32, (ROWS, HEAD), 1)
    diagonal = rows == lanes

    def score(part):
        wait_bytes(q_parts[part].at[others], qf_sem.at[part])
        for rank, (near, side) in enumerate(places):
            q_cat[pl.ds(rank * ROWS, ROWS), :] = q_parts[part][:, near, side].reshape(ROWS, HEAD)
        for block in range(GROUPS):
            below = pl.ds(block * ROWS, (GROUPS - block) * ROWS)
            span = pl.ds(block * BLOCK, BLOCK)
            scores[below, span] = lax.dot_general(
                q_cat[below, :], k_cat[span, :], (((1,), (1,)), ((), ())), preferred_element_type=jnp.float32
            )
        peaks = []
        for rank in range(GROUPS):
            own = pl.ds(rank * ROWS, ROWS)
            strips = [scores[own, pl.ds(i * HEAD, HEAD)] for i in range((rank + 1) * BLOCK // HEAD)]
            peak = jnp.max(functools.reduce(jnp.maximum, strips), axis=1, keepdims=True)
            peaks.append(peak)
            for block in range(rank + 1):
                span = pl.ds(block * BLOCK, BLOCK)
                weights[own, span] = jnp.exp2((scores[own, span] - peak) * SCALE).astype(jnp.bfloat16)
        return peaks

    def attend(part, peaks):
        for block in range(GROUPS):
            below = pl.ds(block * ROWS, (GROUPS - block) * ROWS)
            span = pl.ds(block * BLOCK, BLOCK)
            product = jnp.dot(weights[below, span], v_cat[span, :], preferred_element_type=jnp.float32)
            if block == 0:
                summed[below, :] = product
            else:
                summed[below, :] += product
        for rank in range(GROUPS):
            own = pl.ds(rank * ROWS, ROWS)
            total = summed[own, HEAD:]
            part_out[part, :, rank] = (summed[own, :HEAD] / total).astype(jnp.bfloat16).reshape(SQUARE, TOK, HEAD)
            logs = peaks[rank] * SCALE + jnp.log2(total)
            stats[part, 0, pl.ds(rank, 1), :] = jnp.sum(jnp.where(diagonal, logs, 0.0), axis=0, keepdims=True)
        for step in ACROSS_FIRST:
            pltpu.make_async_remote_copy(
                src_ref=part_out.at[part, step],
                dst_ref=part_in.at[part, step - 1],
                send_sem=send_sem.at[6],
                recv_sem=o_sem.at[part],
                device_id=query_square[step - 1],
                device_id_type=MESH,
            ).start()
            pltpu.make_async_remote_copy(
                src_ref=stats.at[part, 0],
                dst_ref=stats.at[part, step],
                send_sem=send_sem.at[7],
                recv_sem=s_sem.at[part],
                device_id=query_square[step - 1],
                device_id_type=MESH,
            ).start()

    own_rows = lax.broadcasted_iota(jnp.int32, (TOK, HEAD), 0)
    own_lanes = lax.broadcasted_iota(jnp.int32, (TOK, HEAD), 1)

    def merge(part):
        wait_bytes(part_in.at[part], o_sem.at[part])
        wait_bytes(stats.at[part, others], s_sem.at[part])
        for rank in range(GROUPS):
            logs = []
            for step in range(SQUARE):
                line = stats[part, step, pl.ds(rank, 1), :]
                picked = jnp.where(own_lanes == own_rows + step * TOK, line, 0.0)
                logs.append(jnp.sum(picked, axis=1, keepdims=True))
            top = functools.reduce(jnp.maximum, logs)
            shares = [jnp.exp2(log - top) for log in logs]
            whole = functools.reduce(jnp.add, shares)
            value = part_out[part, 0, rank].astype(jnp.float32) * (shares[0] / whole)
            for step in range(1, SQUARE):
                value = value + part_in[part, step - 1, rank].astype(jnp.float32) * (shares[step] / whole)
            merged[part, rank] = value.astype(jnp.bfloat16)
        for g in range(GROUPS):
            row = gate[pl.ds(levels_ref[g], 1), :]
            done = merged[part, ids_ref[g]].astype(jnp.float32) * row
            final[part, g] = done.astype(jnp.bfloat16)

    def give(part):
        for place in range(ZLO):
            from_z = lax.rem(z + Z + distance(part, place), Z)
            lo, hi = lax.rem(from_z, ZLO), lax.div(from_z, ZLO)
            for side in range(2):
                tile = final.at[part, lo * 2 + side]
                to_lo, to_core = (lo, 1) if side == 0 else (lax.rem(lo + 1, ZLO), 0)

                def send():
                    pltpu.make_async_remote_copy(
                        src_ref=tile,
                        dst_ref=out_ref.at[:, column(head)],
                        send_sem=send_sem.at[8],
                        recv_sem=f_sem,
                        device_id=(to_lo * 2 + to_core, (x * 4 + y) * 4 + hi),
                        device_id_type=MESH,
                    ).start()

                def keep():
                    pltpu.make_async_copy(tile, out_ref.at[:, column(head)], f_sem).start()

                if part < 2:
                    send()
                else:
                    here = jnp.logical_and(hi * ZLO + to_lo == z, core == to_core)
                    pl.when(jnp.logical_not(here))(send)
                    pl.when(here)(keep)

    peaks = score(0)
    v_cat[:, HEAD:] = jnp.ones((GROUPS * BLOCK, HEAD), jnp.bfloat16)
    wait_bytes(v_all.at[others], vf_sem)
    for rank, (near, side) in enumerate(places):
        v_cat[pl.ds(rank * BLOCK, BLOCK), :HEAD] = v_all[:, :, near, side].reshape(BLOCK, HEAD)
    attend(0, peaks)
    attend(1, score(1))
    attend(2, score(2))
    merge(0)
    give(0)
    attend(3, score(3))
    sent += [(part_in, 6), (stats.at[:, others], 7), (k_in.at[:, pl.ds(0, (2 * Z - 1) * HEAD)], 8)]
    for part in range(1, PARTS):
        merge(part)
        give(part)
    for ref, number in sent:
        wait_bytes(ref, send_sem.at[number])
    wait_bytes(out_ref, f_sem)


def local(queries, key_states, value_states, gate_table, noise_levels, group_ids):
    bf16, f32 = jnp.bfloat16, jnp.float32
    held = (SQUARE, PARTS, ZLO, 2, TOK, HEAD)
    every = GROUPS * BLOCK
    return pl.pallas_call(
        kernel,
        out_shape=jax.ShapeDtypeStruct((TOK, HEADS * HEAD), bf16),
        in_specs=[pl.BlockSpec(memory_space=pltpu.SMEM)] * 2 + [pl.BlockSpec(memory_space=pl.ANY)] * 4,
        out_specs=pl.BlockSpec(memory_space=pltpu.VMEM),
        scratch_shapes=[
            pltpu.VMEM((TOK, HEADS * HEAD), bf16),
            pltpu.VMEM((TOK, HEADS * HEAD), bf16),
            pltpu.VMEM((TOK, HEADS * HEAD), bf16),
            pltpu.VMEM((32, HEAD), f32),
            *[pltpu.VMEM((SQUARE, ZLO, 2, TOK, HEAD), bf16)] * PARTS,
            pltpu.VMEM(held, bf16),
            pltpu.VMEM(held, bf16),
            pltpu.VMEM((GROUPS * ROWS, HEAD), bf16),
            pltpu.VMEM((every, HEAD), bf16),
            pltpu.VMEM((every, 2 * HEAD), bf16),
            pltpu.VMEM((GROUPS * ROWS, every), f32),
            pltpu.VMEM((GROUPS * ROWS, every), bf16),
            pltpu.VMEM((GROUPS * ROWS, 2 * HEAD), f32),
            pltpu.VMEM((PARTS, SQUARE, GROUPS, TOK, HEAD), bf16),
            pltpu.VMEM((PARTS, SQUARE - 1, GROUPS, TOK, HEAD), bf16),
            pltpu.VMEM((PARTS, SQUARE, GROUPS, HEAD), f32),
            pltpu.VMEM((PARTS, GROUPS, TOK, HEAD), bf16),
            pltpu.VMEM((PARTS, GROUPS, TOK, HEAD), bf16),
            pltpu.SemaphoreType.DMA((4,)),
            pltpu.SemaphoreType.DMA((PARTS,)),
            pltpu.SemaphoreType.DMA((PARTS,)),
            pltpu.SemaphoreType.DMA((PARTS,)),
            pltpu.SemaphoreType.DMA,
            pltpu.SemaphoreType.DMA((PARTS,)),
            pltpu.SemaphoreType.DMA,
            pltpu.SemaphoreType.DMA((PARTS,)),
            pltpu.SemaphoreType.DMA((PARTS,)),
            pltpu.SemaphoreType.DMA,
            pltpu.SemaphoreType.DMA((9,)),
        ],
        compiler_params=pltpu.CompilerParams(
            collective_id=0, has_side_effects=True, vmem_limit_bytes=56 * 2**20
        ),
    )(noise_levels, group_ids, queries, key_states, value_states, gate_table)


def solution(mesh):
    placed = (
        P(("group", "ctx"), None),
        P(("group", "ctx"), None),
        P(("group", "ctx"), None),
        P(),
        P(),
        P(),
    )
    return jax.shard_map(
        local, mesh=mesh, in_specs=placed, out_specs=P(("group", "ctx"), None), check_vma=False
    )
```

```python
import functools
import math

import jax
import jax.numpy as jnp
from jax import lax
from jax.experimental import pallas as pl
from jax.experimental.pallas import tpu as pltpu
from jax.sharding import PartitionSpec as P

HEADS = 32
HEAD = 128
GROUPS = 8
TOK = 16
Z = 16
ZLO = 4
SQUARE = 4
PARTS = 4
ROWS = SQUARE * TOK
BLOCK = PARTS * ROWS
ACROSS_FIRST = (3, 1, 2)
SCALE = math.log2(math.e) / math.sqrt(HEAD)
MESH = pl.DeviceIdType.MESH


def kernel(
    levels_ref, ids_ref, q_ref, k_ref, v_ref, gate_ref, out_ref,
    q_in, k_in, v_in, gate, q_0, q_1, q_2, q_3, k_all, v_all, q_cat, k_cat, v_cat, scores, weights, summed,
    part_out, part_in, stats, merged, final,
    load_sem, kz_sem, qz_sem, vz_sem, kf_sem, qf_sem, vf_sem, o_sem, s_sem, f_sem, send_sem,
):
    group, ctx = lax.axis_index("group"), lax.axis_index("ctx")
    zlo, core = lax.div(group, 2), lax.rem(group, 2)
    x, y, zhi = lax.div(ctx, 16), lax.rem(lax.div(ctx, 4), 4), lax.rem(ctx, 4)
    z = zhi * ZLO + zlo

    def device(to_x, to_y, to_z, to_core):
        return (lax.rem(to_z, ZLO) * 2 + to_core, (to_x * 4 + to_y) * 4 + lax.div(to_z, ZLO))

    def column(head):
        return pl.ds(pl.multiple_of(head * HEAD, HEAD), HEAD)

    def square(shift):
        def partner(position):
            moved = lax.rem(position + shift, 4)
            return lax.rem(moved + 1 - 2 * lax.rem(moved, 2) + 4 - shift, 4)

        to_x, to_y = partner(x), partner(y)
        return [device(to_x, y, z, core), device(x, to_y, z, core), device(to_x, to_y, z, core)]

    key_square, query_square = square(1 - core), square(core)

    head = z * 2 + core
    loads = [
        pltpu.make_async_copy(k_ref, k_in, load_sem.at[0]),
        pltpu.make_async_copy(v_ref, v_in, load_sem.at[1]),
        pltpu.make_async_copy(q_ref, q_in, load_sem.at[2]),
        pltpu.make_async_copy(gate_ref.at[:, column(head)], gate, load_sem.at[3]),
    ]
    for load in loads:
        load.start()

    barrier = pltpu.get_barrier_semaphore()
    for peer in query_square + key_square:
        pl.semaphore_signal(barrier, inc=1, device_id=peer, device_id_type=MESH)

    def greet(i, carry):
        target = device(x, y, lax.rem(z + lax.div(i, 2), Z), lax.rem(core + i, 2))
        pl.semaphore_signal(barrier, inc=1, device_id=target, device_id_type=MESH)
        return carry

    lax.fori_loop(1, 2 * Z, greet, 0)
    for load in loads:
        load.wait()
    pl.semaphore_wait(barrier, 2 * Z - 1 + 2 * (SQUARE - 1))

    def wait_bytes(ref, sem):
        pltpu.make_async_copy(ref, ref, sem).wait()

    sent = []
    q_parts = (q_0, q_1, q_2, q_3)

    def distance(part, place):
        odd = (place + part) % 2
        return place + (8 - 4 * odd if part < 2 else 4 * odd - 4)

    def spread(source, tile, arrived, number, part):
        for place in range(ZLO):
            to_z = lax.rem(z + Z - distance(part, place), Z)
            for to_core in (core, 1 - core):
                if distance(part, place) == 0 and to_core is core:
                    pltpu.make_async_copy(source.at[:, column(head)], tile(place), arrived).start()
                    continue
                pltpu.make_async_remote_copy(
                    src_ref=source.at[:, column(to_z * 2 + to_core)],
                    dst_ref=tile(place),
                    send_sem=send_sem.at[number],
                    recv_sem=arrived,
                    device_id=device(x, y, to_z, to_core),
                    device_id_type=MESH,
                ).start()

    for part in (1, 0):
        spread(k_in, lambda place: k_all.at[0, part, place, core], kz_sem.at[part], 0, part)
    for part in (3, 2):
        spread(k_in, lambda place: k_all.at[0, part, place, core], kz_sem.at[part], 0, part)
    for part in (1, 0):
        spread(v_in, lambda place: v_all.at[0, part, place, core], vz_sem.at[part], 1, part)
    for part in (3, 2):
        spread(v_in, lambda place: v_all.at[0, part, place, core], vz_sem.at[part], 1, part)

    def spread_queries(parts):
        for part in parts:
            spread(q_in, lambda place: q_parts[part].at[0, place, core], qz_sem.at[part], 2, part)

    sent += [(source.at[:, pl.ds(0, (2 * Z - 1) * HEAD)], number) for number, source in enumerate((k_in, v_in, q_in))]

    others = pl.ds(1, SQUARE - 1)

    def pass_on(source, target_ref, target, number, receive):
        pltpu.make_async_remote_copy(
            src_ref=source,
            dst_ref=target_ref,
            send_sem=send_sem.at[number],
            recv_sem=receive,
            device_id=target,
            device_id_type=MESH,
        ).start()

    def pass_part(buffer, part, arrived, number, receive):
        wait_bytes(buffer.at[0, part], arrived.at[part])
        for step in ACROSS_FIRST:
            pass_on(buffer.at[0, part], buffer.at[step, part], key_square[step - 1], number, receive)

    def pass_queries(part):
        queries = q_parts[part]
        wait_bytes(queries.at[0], qz_sem.at[part])
        for step in ACROSS_FIRST:
            pass_on(queries.at[0], queries.at[step], query_square[step - 1], 5, qf_sem.at[part])

    for part in (1, 0):
        pass_part(k_all, part, kz_sem, 3, kf_sem)
    for part in (3, 2):
        pass_part(k_all, part, kz_sem, 3, kf_sem)
    spread_queries((0, 1))
    for part in (1, 0):
        pass_part(v_all, part, vz_sem, 4, vf_sem)
    for part in (3, 2):
        pass_part(v_all, part, vz_sem, 4, vf_sem)
    spread_queries((2, 3))
    for part in range(PARTS - 1):
        pass_queries(part)

    def holder(rank):
        found = jnp.int32(0)
        for g in range(GROUPS):
            found = found + jnp.where(ids_ref[g] == rank, jnp.int32(g), jnp.int32(0))
        return found

    ranked = [holder(rank) for rank in range(GROUPS)]
    places = [(lax.rem(lax.div(g, 2) - zlo + ZLO, ZLO), lax.rem(g, 2)) for g in ranked]

    wait_bytes(k_all.at[others], kf_sem)
    for rank, (near, side) in enumerate(places):
        k_cat[pl.ds(rank * BLOCK, BLOCK), :] = k_all[:, :, near, side].reshape(BLOCK, HEAD)
    pass_queries(PARTS - 1)
    sent += [(k_all.at[others], 3), (v_all.at[others], 4), (k_all.at[others], 5)]

    rows = lax.broadcasted_iota(jnp.int32, (ROWS, HEAD), 0)
    lanes = lax.broadcasted_iota(jnp.int32, (ROWS, HEAD), 1)
    diagonal = rows == lanes

    def score(part):
        wait_bytes(q_parts[part].at[others], qf_sem.at[part])
        for rank, (near, side) in enumerate(places):
            q_cat[pl.ds(rank * ROWS, ROWS), :] = q_parts[part][:, near, side].reshape(ROWS, HEAD)
        for block in range(GROUPS):
            below = pl.ds(block * ROWS, (GROUPS - block) * ROWS)
            span = pl.ds(block * BLOCK, BLOCK)
            scores[below, span] = lax.dot_general(
                q_cat[below, :], k_cat[span, :], (((1,), (1,)), ((), ())), preferred_element_type=jnp.float32
            )
        peaks = []
        for rank in range(GROUPS):
            own = pl.ds(rank * ROWS, ROWS)
            strips = [scores[own, pl.ds(i * HEAD, HEAD)] for i in range((rank + 1) * BLOCK // HEAD)]
            peak = jnp.max(functools.reduce(jnp.maximum, strips), axis=1, keepdims=True)
            peaks.append(peak)
            for block in range(rank + 1):
                span = pl.ds(block * BLOCK, BLOCK)
                weights[own, span] = jnp.exp2((scores[own, span] - peak) * SCALE).astype(jnp.bfloat16)
        return peaks

    def attend(part, peaks):
        for block in range(GROUPS):
            below = pl.ds(block * ROWS, (GROUPS - block) * ROWS)
            span = pl.ds(block * BLOCK, BLOCK)
            product = jnp.dot(weights[below, span], v_cat[span, :], preferred_element_type=jnp.float32)
            if block == 0:
                summed[below, :] = product
            else:
                summed[below, :] += product
        for rank in range(GROUPS):
            own = pl.ds(rank * ROWS, ROWS)
            total = summed[own, HEAD:]
            part_out[part, :, rank] = (summed[own, :HEAD] / total).astype(jnp.bfloat16).reshape(SQUARE, TOK, HEAD)
            logs = peaks[rank] * SCALE + jnp.log2(total)
            stats[part, 0, pl.ds(rank, 1), :] = jnp.sum(jnp.where(diagonal, logs, 0.0), axis=0, keepdims=True)
        for step in ACROSS_FIRST:
            pltpu.make_async_remote_copy(
                src_ref=part_out.at[part, step],
                dst_ref=part_in.at[part, step - 1],
                send_sem=send_sem.at[6],
                recv_sem=o_sem.at[part],
                device_id=query_square[step - 1],
                device_id_type=MESH,
            ).start()
            pltpu.make_async_remote_copy(
                src_ref=stats.at[part, 0],
                dst_ref=stats.at[part, step],
                send_sem=send_sem.at[7],
                recv_sem=s_sem.at[part],
                device_id=query_square[step - 1],
                device_id_type=MESH,
            ).start()

    own_rows = lax.broadcasted_iota(jnp.int32, (TOK, HEAD), 0)
    own_lanes = lax.broadcasted_iota(jnp.int32, (TOK, HEAD), 1)

    def merge(part):
        wait_bytes(part_in.at[part], o_sem.at[part])
        wait_bytes(stats.at[part, others], s_sem.at[part])
        for rank in range(GROUPS):
            logs = []
            for step in range(SQUARE):
                line = stats[part, step, pl.ds(rank, 1), :]
                picked = jnp.where(own_lanes == own_rows + step * TOK, line, 0.0)
                logs.append(jnp.sum(picked, axis=1, keepdims=True))
            top = functools.reduce(jnp.maximum, logs)
            shares = [jnp.exp2(log - top) for log in logs]
            whole = functools.reduce(jnp.add, shares)
            value = part_out[part, 0, rank].astype(jnp.float32) * (shares[0] / whole)
            for step in range(1, SQUARE):
                value = value + part_in[part, step - 1, rank].astype(jnp.float32) * (shares[step] / whole)
            merged[part, rank] = value.astype(jnp.bfloat16)
        for g in range(GROUPS):
            row = gate[pl.ds(levels_ref[g], 1), :]
            done = merged[part, ids_ref[g]].astype(jnp.float32) * row
            final[part, g] = done.astype(jnp.bfloat16)

    def give(part):
        for place in range(ZLO):
            from_z = lax.rem(z + Z + distance(part, place), Z)
            lo, hi = lax.rem(from_z, ZLO), lax.div(from_z, ZLO)
            for side in range(2):
                tile = final.at[part, lo * 2 + side]
                to_lo, to_core = (lo, 1) if side == 0 else (lax.rem(lo + 1, ZLO), 0)

                def send():
                    pltpu.make_async_remote_copy(
                        src_ref=tile,
                        dst_ref=out_ref.at[:, column(head)],
                        send_sem=send_sem.at[8],
                        recv_sem=f_sem,
                        device_id=(to_lo * 2 + to_core, (x * 4 + y) * 4 + hi),
                        device_id_type=MESH,
                    ).start()

                def keep():
                    pltpu.make_async_copy(tile, out_ref.at[:, column(head)], f_sem).start()

                if part < 2:
                    send()
                else:
                    here = jnp.logical_and(hi * ZLO + to_lo == z, core == to_core)
                    pl.when(jnp.logical_not(here))(send)
                    pl.when(here)(keep)

    peaks = score(0)
    v_cat[:, HEAD:] = jnp.ones((GROUPS * BLOCK, HEAD), jnp.bfloat16)
    wait_bytes(v_all.at[others], vf_sem)
    for rank, (near, side) in enumerate(places):
        v_cat[pl.ds(rank * BLOCK, BLOCK), :HEAD] = v_all[:, :, near, side].reshape(BLOCK, HEAD)
    attend(0, peaks)
    attend(1, score(1))
    attend(2, score(2))
    merge(0)
    give(0)
    attend(3, score(3))
    sent += [(part_in, 6), (stats.at[:, others], 7), (k_in.at[:, pl.ds(0, (2 * Z - 1) * HEAD)], 8)]
    for part in range(1, PARTS):
        merge(part)
        give(part)
    for ref, number in sent:
        wait_bytes(ref, send_sem.at[number])
    wait_bytes(out_ref, f_sem)


def local(queries, key_states, value_states, gate_table, noise_levels, group_ids):
    bf16, f32 = jnp.bfloat16, jnp.float32
    held = (SQUARE, PARTS, ZLO, 2, TOK, HEAD)
    every = GROUPS * BLOCK
    return pl.pallas_call(
        kernel,
        out_shape=jax.ShapeDtypeStruct((TOK, HEADS * HEAD), bf16),
        in_specs=[pl.BlockSpec(memory_space=pltpu.SMEM)] * 2 + [pl.BlockSpec(memory_space=pl.ANY)] * 4,
        out_specs=pl.BlockSpec(memory_space=pl.ANY),
        scratch_shapes=[
            pltpu.VMEM((TOK, HEADS * HEAD), bf16),
            pltpu.VMEM((TOK, HEADS * HEAD), bf16),
            pltpu.VMEM((TOK, HEADS * HEAD), bf16),
            pltpu.VMEM((32, HEAD), f32),
            *[pltpu.VMEM((SQUARE, ZLO, 2, TOK, HEAD), bf16)] * PARTS,
            pltpu.VMEM(held, bf16),
            pltpu.VMEM(held, bf16),
            pltpu.VMEM((GROUPS * ROWS, HEAD), bf16),
            pltpu.VMEM((every, HEAD), bf16),
            pltpu.VMEM((every, 2 * HEAD), bf16),
            pltpu.VMEM((GROUPS * ROWS, every), f32),
            pltpu.VMEM((GROUPS * ROWS, every), bf16),
            pltpu.VMEM((GROUPS * ROWS, 2 * HEAD), f32),
            pltpu.VMEM((PARTS, SQUARE, GROUPS, TOK, HEAD), bf16),
            pltpu.VMEM((PARTS, SQUARE - 1, GROUPS, TOK, HEAD), bf16),
            pltpu.VMEM((PARTS, SQUARE, GROUPS, HEAD), f32),
            pltpu.VMEM((PARTS, GROUPS, TOK, HEAD), bf16),
            pltpu.VMEM((PARTS, GROUPS, TOK, HEAD), bf16),
            pltpu.SemaphoreType.DMA((4,)),
            pltpu.SemaphoreType.DMA((PARTS,)),
            pltpu.SemaphoreType.DMA((PARTS,)),
            pltpu.SemaphoreType.DMA((PARTS,)),
            pltpu.SemaphoreType.DMA,
            pltpu.SemaphoreType.DMA((PARTS,)),
            pltpu.SemaphoreType.DMA,
            pltpu.SemaphoreType.DMA((PARTS,)),
            pltpu.SemaphoreType.DMA((PARTS,)),
            pltpu.SemaphoreType.DMA,
            pltpu.SemaphoreType.DMA((9,)),
        ],
        compiler_params=pltpu.CompilerParams(
            collective_id=0, has_side_effects=True, vmem_limit_bytes=56 * 2**20
        ),
    )(noise_levels, group_ids, queries, key_states, value_states, gate_table)


def solution(mesh):
    placed = (
        P(("group", "ctx"), None),
        P(("group", "ctx"), None),
        P(("group", "ctx"), None),
        P(),
        P(),
        P(),
    )
    return jax.shard_map(
        local, mesh=mesh, in_specs=placed, out_specs=P(("group", "ctx"), None), check_vma=False
    )
```
